32 devices in a mesh: outer: 2 (over x), dp: 16 (over z, y, core).
Axes of the slice: x: 2, y: 2, z: 4, core: 2. Of those that a mesh axis runs over, the one named last changes fastest.
Arguments:
- grads: float32 [2, 2, 1024, 576], P('outer', None, 'dp'), may hold values from -64 to 64
- momentum: float32 [2, 1024, 576], P(None, 'dp'), may hold values from -4 to 4
Outputs:
- momentum_new: float32 [2, 1024, 576], P(None, 'dp')
- update: float32 [2, 1024, 576], P(None, 'dp')
The draws below stay inside these ranges and needn't reach their ends.
All inputs are finite; a program needn't handle non-finite values.
Results may differ from the reference program's by a relative error of at most 0.0057.
Values may be sent and summed in bfloat16 or wider, within the bound.
No kernel may reach another device: no remote copies, remote signals or barrier semaphores. Data moves between devices by JAX's collectives and lax.ppermute only.
A program may use at most 64 MiB of HBM per device.

```python
import math
import jax
import jax.numpy as jnp
from jax import lax

R = 1024
C = 576
ITERS = 2
PODS = 2
MATS = 2


def draw_grads(key, part):
    key_noise, key_row, key_col = jax.random.split(key, 3)
    noise = jax.random.normal(key_noise, (PODS, MATS, R, C), jnp.float32)
    row_top = math.log(10.0)
    noise = jnp.clip(noise, -4.0, 4.0)
    row_scale = jnp.exp(row_top * jax.random.uniform(key_row, (1, MATS, R, 1), jnp.float32))
    col_scale = jnp.exp(math.log(10.0) * jax.random.uniform(key_col, (1, MATS, 1, C), jnp.float32))
    trend = jnp.exp(math.log(3.0) * jnp.arange(R, dtype=jnp.float32) / (R - 1)).reshape(1, 1, R, 1)
    return noise * row_scale * col_scale * trend / 30.0


def steps_of(stream_key, extent, cuts, least, high):
    def one(axis_at, shards_of):
        heights = jax.random.uniform(jax.random.fold_in(jax.random.fold_in(stream_key, 6), axis_at), (shards_of,), jnp.float32, least / len(cuts), high / len(cuts))
        return jnp.repeat(jnp.exp(heights), extent[axis_at] // shards_of).reshape((-1,) + (1,) * (len(extent) - axis_at - 1))

    loudness = one(*cuts[0])
    for cut in cuts[1:]:
        loudness = loudness * one(*cut)
    return loudness


def centred(rng, dims, deviation, bound, pieces=(), kind=jnp.bfloat16):
    array = deviation * jax.random.normal(rng, dims, jnp.float32)
    if pieces:
        array = array * steps_of(rng, dims, pieces, -0.22, 0.18)
    return jnp.clip(array, -bound, bound).astype(kind)


def setup_inputs(seed: int = 0) -> dict:
    key_of = jax.random.split(jax.random.key(seed), 3)
    return {
        "grads": draw_grads(jax.random.fold_in(key_of[2], 71), 0),
        "momentum": centred(key_of[1], (MATS, R, C), 0.5, 4.0, ((1, 16),), jnp.float32),
    }


coef_a = 3.4445
coef_b = -4.775
coef_c = 2.0315
momentum_rate = 0.95
epsilon = 1e-06

def gram_product(matrix):
    return lax.dot_general(matrix, matrix, (((0,), (0,)), ((), ())), preferred_element_type=jnp.float32)

def newton_steps(matrix):
    for iteration in range(ITERS):
        gram_matrix = gram_product(matrix).astype(jnp.bfloat16)
        squared = jnp.dot(gram_matrix, gram_matrix, preferred_element_type=jnp.float32)
        polynomial = (coef_b * gram_matrix.astype(jnp.float32) + coef_c * squared).astype(jnp.bfloat16)
        mixed = jnp.dot(matrix, polynomial, preferred_element_type=jnp.float32)
        matrix = (coef_a * matrix.astype(jnp.float32) + mixed).astype(jnp.bfloat16)
    return matrix

def orthogonalize(steering):
    values = steering.astype(jnp.float32)
    norm_value = jnp.sqrt(jnp.sum(values * values))
    start = (values / (norm_value + epsilon)).astype(jnp.bfloat16)
    return newton_steps(start)

def reference(grads, momentum):
    summed = lax.optimization_barrier(jnp.sum(grads, axis=0))
    momentum_new = momentum_rate * momentum + summed
    steering = (summed + momentum_rate * momentum_new).astype(jnp.bfloat16)
    orthogonal = lax.map(orthogonalize, steering)
    update_scale = 0.2 * math.sqrt(max(R, C))
    return (momentum_new, update_scale * orthogonal.astype(jnp.float32))
```

```python
import functools
import math

import jax
import jax.numpy as jnp
from jax import lax
from jax.experimental import pallas as pl
from jax.experimental.pallas import tpu as pltpu
from jax.sharding import PartitionSpec as P

ITERS = 2

coef_a = 3.4445
coef_b = -4.775
coef_c = 2.0315
momentum_rate = 0.95
epsilon = 1e-06

BF16 = jnp.bfloat16
F32 = jnp.float32
VMEM = pl.BlockSpec(memory_space=pltpu.VMEM)
SMEM = pl.BlockSpec(memory_space=pltpu.SMEM)
PARAMS = pltpu.CompilerParams(vmem_limit_bytes=40 * 1024 * 1024)


def dot(left, right):
    return jnp.dot(left, right, preferred_element_type=F32)


def gram_product(matrix):
    return lax.dot_general(matrix, matrix, (((0,), (0,)), ((), ())), preferred_element_type=F32)


def trace_of(gram):
    size = gram.shape[0]
    total = jnp.zeros((1, 1), F32)
    for at in range(0, size, 128):
        part = min(128, size - at)
        block = gram[at : at + part, at : at + part]
        row = lax.broadcasted_iota(jnp.int32, (part, part), 0)
        column = lax.broadcasted_iota(jnp.int32, (part, part), 1)
        total = total + jnp.sum(jnp.where(row == column, block, 0.0), keepdims=True)
    return total


def own_rows(gram_raw, rows):
    inverse = 1.0 / (jnp.sqrt(trace_of(gram_raw)) + epsilon)
    gram = (gram_raw * (inverse * inverse)).astype(BF16)
    polynomial = (coef_b * gram.astype(F32) + coef_c * dot(gram, gram)).astype(BF16)

    def by_q(value):
        return coef_a * value.astype(F32) + dot(value, polynomial)

    def by_second_gram(value):
        return by_q(dot(by_q(value).astype(BF16), gram).astype(BF16)).astype(BF16)

    start = (rows.astype(F32) * inverse).astype(BF16)
    first = by_q(start)
    once = by_second_gram(first.astype(BF16))
    twice = by_second_gram(once)
    return coef_a * first + coef_b * once.astype(F32) + coef_c * twice.astype(F32)


def finish_kernel(rows_ref, *refs):
    blocks, out_ref, held = refs[:-2], refs[-2], refs[-1]
    at = 0
    for block in blocks:
        held[at : at + block.shape[0], :] = block[...]
        at += block.shape[0]
    out_ref[...] = own_rows(gram_product(held[...]), rows_ref[...]).astype(BF16)


def finish(rows, blocks):
    height = sum(block.shape[0] for block in blocks)
    width = rows.shape[1]
    return pl.pallas_call(
        finish_kernel,
        out_shape=jax.ShapeDtypeStruct(rows.shape, BF16),
        in_specs=[VMEM] * (1 + len(blocks)),
        out_specs=VMEM,
        scratch_shapes=[pltpu.VMEM((height, width), BF16)],
        compiler_params=PARAMS,
    )(rows, *blocks)


def exchange(value, axis, distance):
    size = lax.axis_size(axis)
    return lax.ppermute(value, axis, [(at, at ^ distance) for at in range(size)])


def gather_blocks(block):
    size = lax.axis_size("dp")
    if size != 16:
        return [lax.all_gather(block, "dp", axis=0, tiled=True)]
    z2 = exchange(block, "dp", 8)
    z1 = exchange(block, "dp", 4)
    y0 = exchange(block, "dp", 2)
    z3 = exchange(z2, "dp", 4)
    y1 = exchange(z1, "dp", 2)
    y2 = exchange(z2, "dp", 2)
    y3 = exchange(z3, "dp", 2)
    mine = [block, y0, z1, z2, y1, z3, y2, y3]
    return mine + [exchange(value, "dp", 1) for value in mine]


def two_pods(local, momentum):
    pod = lax.axis_index("outer")
    update_scale = 0.2 * math.sqrt(max(local.shape[1] * lax.axis_size("dp"), local.shape[2]))
    first = pod == 0

    def pick(array, other=False):
        return jnp.where(first != other, array[0], array[1])

    away = pick(local, True).astype(BF16)
    kept = pick(local).astype(BF16)
    arrived = exchange(away, "outer", 1)
    summed = kept.astype(F32) + arrived.astype(F32)
    mine_new = momentum_rate * pick(momentum) + summed
    steering = (summed + momentum_rate * mine_new).astype(BF16)

    arrived_too = exchange(kept, "outer", 1)
    other_new = momentum_rate * pick(momentum, True) + (away.astype(F32) + arrived_too.astype(F32))
    momentum_new = jnp.where(first, jnp.stack([mine_new, other_new]), jnp.stack([other_new, mine_new]))

    mine = finish(steering, gather_blocks(steering))
    other = exchange(mine, "outer", 1)
    both = jnp.where(first, jnp.stack([mine, other]), jnp.stack([other, mine]))
    return momentum_new, update_scale * both.astype(F32)


def any_pods(local, momentum):
    pods = lax.axis_size("outer")
    pod = lax.axis_index("outer")
    count, rows, width = local.shape
    per_pod = count // pods
    update_scale = 0.2 * math.sqrt(max(rows * lax.axis_size("dp"), width))
    summed = lax.psum(local, "outer")
    momentum_new = momentum_rate * momentum + summed
    steering = summed + momentum_rate * momentum_new
    steering = lax.dynamic_slice_in_dim(steering, pod * per_pod, per_pod, 0).astype(BF16)
    mine = jnp.stack([finish(steering[at], gather_blocks(steering[at])) for at in range(per_pod)])
    gathered = lax.all_gather(mine, "outer", axis=0, tiled=True)
    return momentum_new, update_scale * gathered.astype(F32)


def per_device(grads, momentum):
    local = grads[0]
    if lax.axis_size("outer") == 2 and local.shape[0] == 2:
        return two_pods(local, momentum)
    return any_pods(local, momentum)


def solution(mesh):
    in_specs = (P("outer", None, "dp", None), P(None, "dp", None))
    out_specs = (P(None, "dp", None), P(None, "dp", None))
    return jax.shard_map(
        per_device, mesh=mesh, in_specs=in_specs, out_specs=out_specs, check_vma=False
    )
```

```python
import functools
import math

import jax
import jax.numpy as jnp
from jax import lax
from jax.experimental import pallas as pl
from jax.experimental.pallas import tpu as pltpu
from jax.sharding import PartitionSpec as P

ITERS = 2

coef_a = 3.4445
coef_b = -4.775
coef_c = 2.0315
momentum_rate = 0.95
epsilon = 1e-06

BF16 = jnp.bfloat16
F32 = jnp.float32
VMEM = pl.BlockSpec(memory_space=pltpu.VMEM)
SMEM = pl.BlockSpec(memory_space=pltpu.SMEM)
PARAMS = pltpu.CompilerParams(vmem_limit_bytes=16 * 1024 * 1024)
SMALL = pltpu.CompilerParams(vmem_limit_bytes=4 * 1024 * 1024)


def dot(left, right):
    return jnp.dot(left, right, preferred_element_type=F32)


def gram_product(matrix):
    return lax.dot_general(matrix, matrix, (((0,), (0,)), ((), ())), preferred_element_type=F32)


def trace_of(gram):
    size = gram.shape[0]
    total = jnp.zeros((1, 1), F32)
    for at in range(0, size, 128):
        part = min(128, size - at)
        block = gram[at : at + part, at : at + part]
        row = lax.broadcasted_iota(jnp.int32, (part, part), 0)
        column = lax.broadcasted_iota(jnp.int32, (part, part), 1)
        total = total + jnp.sum(jnp.where(row == column, block, 0.0), keepdims=True)
    return total


def own_rows(gram_raw, rows):
    gram = gram_raw.astype(BF16)
    squared = dot(gram, gram)
    inverse = 1.0 / (jnp.sqrt(trace_of(gram_raw)) + epsilon)
    scale = inverse * inverse
    polynomial = ((coef_b * scale) * gram.astype(F32) + (coef_c * scale * scale) * squared).astype(BF16)

    def by_q(value):
        return coef_a * value.astype(F32) + dot(value, polynomial)

    def by_second_gram(value):
        return by_q((scale * dot(by_q(value).astype(BF16), gram)).astype(BF16)).astype(BF16)

    first = by_q(rows)
    once = by_second_gram(first.astype(BF16))
    twice = by_second_gram(once)
    return inverse * (coef_a * first + coef_b * once.astype(F32) + coef_c * twice.astype(F32))


def pack(value, ref, at=0):
    rows, width = value.shape
    whole = width // 128
    for tile in range(whole):
        ref[at + rows * tile : at + rows * (tile + 1), :] = value[:, 128 * tile : 128 * (tile + 1)]
    rest = value[:, 128 * whole :]
    half = rows // 2
    ref[at + rows * whole : at + rows * whole + half, :] = jnp.concatenate([rest[:half], rest[half:]], axis=1)


def unpack(ref, at, held, to, rows, width):
    whole = width // 128
    for tile in range(whole):
        part = ref[at + rows * tile : at + rows * (tile + 1), :]
        held[to : to + rows, 128 * tile : 128 * (tile + 1)] = part.astype(held.dtype)
    half = rows // 2
    rest = ref[at + rows * whole : at + rows * whole + half, :].astype(held.dtype)
    held[to : to + half, 128 * whole :] = rest[:, :64]
    held[to + half : to + rows, 128 * whole :] = rest[:, 64:]


def unpack_all(blocks, held, rows, width):
    size = rows * width // 128
    to = 0
    for block in blocks:
        for at in range(0, block.shape[0], size):
            unpack(block, at, held, to, rows, width)
            to += rows
    return held[...]


def rows_in(blocks, width):
    return sum(block.shape[0] for block in blocks) * 128 // width


def gram_kernel(rows, more, *refs):
    blocks, out_ref, held = refs[more:-2], refs[-2], refs[-1]
    gram = gram_product(unpack_all(blocks, held, rows, held.shape[1]))
    out_ref[...] = refs[0][...] + gram if more else gram


def gram_of(blocks, rows, width, so_far=None):
    before = [] if so_far is None else [so_far]
    return pl.pallas_call(
        functools.partial(gram_kernel, rows, len(before)),
        out_shape=jax.ShapeDtypeStruct((width, width), F32),
        in_specs=[VMEM] * (len(before) + len(blocks)),
        out_specs=VMEM,
        scratch_shapes=[pltpu.VMEM((rows_in(blocks, width), width), BF16)],
        compiler_params=PARAMS,
    )(*before, *blocks)


def finish_kernel(rows, sum_ref, rows_ref, *refs):
    blocks, out_ref, held, own = refs[:-3], refs[-3], refs[-2], refs[-1]
    unpack(rows_ref, 0, own, 0, rows, own.shape[1])
    gram = sum_ref[...] + gram_product(unpack_all(blocks, held, rows, held.shape[1]))
    pack(own_rows(gram, own[...]).astype(BF16), out_ref)


def finish(so_far, own, blocks, rows, width):
    return pl.pallas_call(
        functools.partial(finish_kernel, rows),
        out_shape=jax.ShapeDtypeStruct(own.shape, BF16),
        in_specs=[VMEM] * (2 + len(blocks)),
        out_specs=VMEM,
        scratch_shapes=[pltpu.VMEM((rows_in(blocks, width), width), BF16), pltpu.VMEM((rows, width), BF16)],
        compiler_params=PARAMS,
    )(so_far, own, *blocks)


def whole_kernel(rows_ref, whole_ref, out_ref):
    out_ref[...] = own_rows(gram_product(whole_ref[...]), rows_ref[...]).astype(BF16)


def whole_finish(own):
    return pl.pallas_call(
        whole_kernel,
        out_shape=jax.ShapeDtypeStruct(own.shape, BF16),
        in_specs=[VMEM] * 2,
        out_specs=VMEM,
        compiler_params=PARAMS,
    )(own, lax.all_gather(own, "dp", axis=0, tiled=True))


def join_kernel(*refs):
    at = 0
    for ref in refs[:-1]:
        refs[-1][at : at + ref.shape[0], :] = ref[...]
        at += ref.shape[0]


def join(blocks):
    height = sum(block.shape[0] for block in blocks)
    return pl.pallas_call(
        join_kernel,
        out_shape=jax.ShapeDtypeStruct((height, 128), BF16),
        in_specs=[VMEM] * len(blocks),
        out_specs=VMEM,
        compiler_params=SMALL,
    )(*blocks)


def exchange(value, axis, distance):
    size = lax.axis_size(axis)
    return lax.ppermute(value, axis, [(at, at ^ distance) for at in range(size)])


def after(value, *others):
    return lax.optimization_barrier((value, *others))[0]


def gather_and_finish(block, kept, rows, width):
    z2 = exchange(block, "dp", 8)
    z1 = exchange(block, "dp", 4)
    y0 = exchange(block, "dp", 2)
    beside = exchange(kept, "outer", 1)
    z2, beside = lax.optimization_barrier((z2, beside))
    z3 = exchange(z2, "dp", 4)
    y1 = exchange(z1, "dp", 2)
    y2 = exchange(z2, "dp", 2)
    y3 = exchange(z3, "dp", 2)
    near = [block, z1, z2]
    near = near + [exchange(v, "dp", 1) for v in near]
    gram = gram_of(near, rows, width)
    far = [y0, z3, y1, y2]
    far = far + [exchange(v, "dp", 1) for v in far]
    return finish(gram, block, far + [y3, exchange(y3, "dp", 1)], rows, width), beside


def away_kernel(grads_ref, away_ref, held, done):
    copy = pltpu.make_async_copy(grads_ref.at[1 - lax.axis_index("outer")], held, done)
    copy.start()
    copy.wait()
    pack(held[...].astype(BF16), away_ref)


def base_kernel(grads_ref, momentum_ref, kept_ref, base_ref, held, done):
    mine = lax.axis_index("outer")
    copies = [
        pltpu.make_async_copy(grads_ref.at[mine], held.at[0], done.at[0]),
        pltpu.make_async_copy(momentum_ref.at[mine], held.at[1], done.at[1]),
    ]
    for copy in copies:
        copy.start()
    for copy in copies:
        copy.wait()
    pack(held[0].astype(BF16), kept_ref)
    pack((1.0 + momentum_rate) * held[0] + (momentum_rate * momentum_rate) * held[1], base_ref)


def steering_kernel(base_ref, arrived_ref, out_ref):
    out_ref[...] = (base_ref[...] + (1.0 + momentum_rate) * arrived_ref[...].astype(F32)).astype(BF16)


def momentum_kernel(momentum_ref, kept_ref, arrived_ref, away_ref, arrived_too_ref, out_ref, held):
    mine = lax.axis_index("outer")
    rows, width = held.shape
    for at, sent, came in ((mine, kept_ref, arrived_ref), (1 - mine, away_ref, arrived_too_ref)):
        unpack(sent[...].astype(F32) + came[...].astype(F32), 0, held, 0, rows, width)
        out_ref[at] = momentum_rate * momentum_ref[at] + held[...]


def update_kernel(scale, own, rows_ref, *refs):
    out_ref, held, done = refs[-3:]
    mine = lax.axis_index("outer")
    unpack(scale * rows_ref[...].astype(F32), 0, held, 0, *held.shape)
    copy = pltpu.make_async_copy(held, out_ref.at[mine if own else 1 - mine], done)
    copy.start()
    copy.wait()


def two_pods(local, momentum):
    _, rows, width = local.shape
    update_scale = 0.2 * math.sqrt(max(rows * lax.axis_size("dp"), width))
    anywhere = pl.BlockSpec(memory_space=pl.ANY)
    one = (rows, width)
    packed = (rows * width // 128, 128)
    rounded = jax.ShapeDtypeStruct(packed, BF16)
    wide = jax.ShapeDtypeStruct(packed, F32)
    both = jax.ShapeDtypeStruct(local.shape, F32)
    away = pl.pallas_call(
        away_kernel,
        out_shape=rounded,
        in_specs=[anywhere],
        out_specs=VMEM,
        scratch_shapes=[pltpu.VMEM(one, F32), pltpu.SemaphoreType.DMA],
        compiler_params=SMALL,
    )(local)
    arrived = exchange(away, "outer", 1)
    kept, base = pl.pallas_call(
        base_kernel,
        out_shape=(rounded, wide),
        in_specs=[anywhere] * 2,
        out_specs=(VMEM, VMEM),
        scratch_shapes=[pltpu.VMEM((2,) + one, F32), pltpu.SemaphoreType.DMA((2,))],
        compiler_params=SMALL,
    )(local, momentum)
    steering = pl.pallas_call(
        steering_kernel, out_shape=rounded, in_specs=[VMEM] * 2, out_specs=VMEM, compiler_params=SMALL
    )(base, arrived)

    mine, arrived_too = gather_and_finish(steering, kept, rows, width)

    momentum_new = pl.pallas_call(
        momentum_kernel,
        out_shape=both,
        in_specs=[VMEM] * 5,
        scratch_shapes=[pltpu.VMEM(one, F32)],
        compiler_params=SMALL,
    )(momentum, kept, arrived, away, arrived_too)

    other = exchange(mine, "outer", 1)
    scratch = [pltpu.VMEM(one, F32), pltpu.SemaphoreType.DMA]
    half = pl.pallas_call(
        functools.partial(update_kernel, update_scale, True),
        out_shape=both,
        in_specs=[VMEM],
        out_specs=anywhere,
        scratch_shapes=scratch,
        compiler_params=SMALL,
    )(mine)
    update = pl.pallas_call(
        functools.partial(update_kernel, update_scale, False),
        out_shape=both,
        in_specs=[VMEM, anywhere],
        out_specs=anywhere,
        scratch_shapes=scratch,
        input_output_aliases={1: 0},
        compiler_params=SMALL,
    )(other, half)
    return momentum_new, update


def any_pods(local, momentum):
    pods = lax.axis_size("outer")
    pod = lax.axis_index("outer")
    count, rows, width = local.shape
    per_pod = count // pods
    update_scale = 0.2 * math.sqrt(max(rows * lax.axis_size("dp"), width))
    summed = lax.psum(local, "outer")
    momentum_new = momentum_rate * momentum + summed
    steering = summed + momentum_rate * momentum_new
    steering = lax.dynamic_slice_in_dim(steering, pod * per_pod, per_pod, 0).astype(BF16)
    mine = jnp.stack([whole_finish(steering[at]) for at in range(per_pod)])
    gathered = lax.all_gather(mine, "outer", axis=0, tiled=True)
    return momentum_new, update_scale * gathered.astype(F32)


def per_device(grads, momentum):
    local = grads[0]
    _, rows, width = local.shape
    halves = width % 128 == 64 and rows % 32 == 0
    if lax.axis_size("outer") == 2 and local.shape[0] == 2 and lax.axis_size("dp") == 16 and halves:
        return two_pods(local, momentum)
    return any_pods(local, momentum)


def solution(mesh):
    in_specs = (P("outer", None, "dp", None), P(None, "dp", None))
    out_specs = (P(None, "dp", None), P(None, "dp", None))
    return jax.shard_map(
        per_device, mesh=mesh, in_specs=in_specs, out_specs=out_specs, check_vma=False
    )
```

```python
import functools
import math

import jax
import jax.numpy as jnp
from jax import lax
from jax.experimental import pallas as pl
from jax.experimental.pallas import tpu as pltpu
from jax.sharding import PartitionSpec as P

ITERS = 2

coef_a = 3.4445
coef_b = -4.775
coef_c = 2.0315
momentum_rate = 0.95
epsilon = 1e-06

BF16 = jnp.bfloat16
F32 = jnp.float32
VMEM = pl.BlockSpec(memory_space=pltpu.VMEM)
SMEM = pl.BlockSpec(memory_space=pltpu.SMEM)
PARAMS = pltpu.CompilerParams(vmem_limit_bytes=16 * 1024 * 1024)
SMALL = pltpu.CompilerParams(vmem_limit_bytes=4 * 1024 * 1024)


def dot(left, right):
    return jnp.dot(left, right, preferred_element_type=F32)


def gram_product(matrix):
    return lax.dot_general(matrix, matrix, (((0,), (0,)), ((), ())), preferred_element_type=F32)


def trace_of(gram):
    size = gram.shape[0]
    total = jnp.zeros((1, 1), F32)
    for at in range(0, size, 128):
        part = min(128, size - at)
        block = gram[at : at + part, at : at + part]
        row = lax.broadcasted_iota(jnp.int32, (part, part), 0)
        column = lax.broadcasted_iota(jnp.int32, (part, part), 1)
        total = total + jnp.sum(jnp.where(row == column, block, 0.0), keepdims=True)
    return total


def own_rows(gram_raw, rows):
    gram = gram_raw.astype(BF16)
    squared = dot(gram, gram)
    inverse = 1.0 / (jnp.sqrt(trace_of(gram_raw)) + epsilon)
    scale = inverse * inverse
    polynomial = ((coef_b * scale) * gram.astype(F32) + (coef_c * scale * scale) * squared).astype(BF16)

    def by_q(value):
        return coef_a * value.astype(F32) + dot(value, polynomial)

    def by_second_gram(value):
        return by_q((scale * dot(by_q(value).astype(BF16), gram)).astype(BF16)).astype(BF16)

    first = by_q(rows)
    once = by_second_gram(first.astype(BF16))
    twice = by_second_gram(once)
    return inverse * (coef_a * first + coef_b * once.astype(F32) + coef_c * twice.astype(F32))


def pack(value, ref, at=0):
    rows, width = value.shape
    whole = width // 128
    for tile in range(whole):
        ref[at + rows * tile : at + rows * (tile + 1), :] = value[:, 128 * tile : 128 * (tile + 1)]
    rest = value[:, 128 * whole :]
    half = rows // 2
    ref[at + rows * whole : at + rows * whole + half, :] = jnp.concatenate([rest[:half], rest[half:]], axis=1)


def unpack(ref, at, held, to, rows, width):
    whole = width // 128
    for tile in range(whole):
        part = ref[at + rows * tile : at + rows * (tile + 1), :]
        held[to : to + rows, 128 * tile : 128 * (tile + 1)] = part.astype(held.dtype)
    half = rows // 2
    rest = ref[at + rows * whole : at + rows * whole + half, :].astype(held.dtype)
    held[to : to + half, 128 * whole :] = rest[:, :64]
    held[to + half : to + rows, 128 * whole :] = rest[:, 64:]


def unpack_all(blocks, held, rows, width):
    size = rows * width // 128
    to = 0
    for block in blocks:
        for at in range(0, block.shape[0], size):
            unpack(block, at, held, to, rows, width)
            to += rows
    return held[...]


def rows_in(blocks, width):
    return sum(block.shape[0] for block in blocks) * 128 // width


def gram_kernel(rows, more, *refs):
    blocks, out_ref, held = refs[more:-2], refs[-2], refs[-1]
    gram = gram_product(unpack_all(blocks, held, rows, held.shape[1]))
    out_ref[...] = refs[0][...] + gram if more else gram


def gram_of(blocks, rows, width, so_far=None):
    before = [] if so_far is None else [so_far]
    return pl.pallas_call(
        functools.partial(gram_kernel, rows, len(before)),
        out_shape=jax.ShapeDtypeStruct((width, width), F32),
        in_specs=[VMEM] * (len(before) + len(blocks)),
        out_specs=VMEM,
        scratch_shapes=[pltpu.VMEM((rows_in(blocks, width), width), BF16)],
        compiler_params=PARAMS,
    )(*before, *blocks)


def finish_kernel(rows, sum_ref, rows_ref, *refs):
    blocks, out_ref, held, own = refs[:-3], refs[-3], refs[-2], refs[-1]
    unpack(rows_ref, 0, own, 0, rows, own.shape[1])
    gram = sum_ref[...] + gram_product(unpack_all(blocks, held, rows, held.shape[1]))
    pack(own_rows(gram, own[...]).astype(BF16), out_ref)


def finish(so_far, own, blocks, rows, width):
    return pl.pallas_call(
        functools.partial(finish_kernel, rows),
        out_shape=jax.ShapeDtypeStruct(own.shape, BF16),
        in_specs=[VMEM] * (2 + len(blocks)),
        out_specs=VMEM,
        scratch_shapes=[pltpu.VMEM((rows_in(blocks, width), width), BF16), pltpu.VMEM((rows, width), BF16)],
        compiler_params=PARAMS,
    )(so_far, own, *blocks)


def whole_kernel(rows_ref, whole_ref, out_ref):
    out_ref[...] = own_rows(gram_product(whole_ref[...]), rows_ref[...]).astype(BF16)


def whole_finish(own):
    return pl.pallas_call(
        whole_kernel,
        out_shape=jax.ShapeDtypeStruct(own.shape, BF16),
        in_specs=[VMEM] * 2,
        out_specs=VMEM,
        compiler_params=PARAMS,
    )(own, lax.all_gather(own, "dp", axis=0, tiled=True))


def join_kernel(*refs):
    at = 0
    for ref in refs[:-1]:
        refs[-1][at : at + ref.shape[0], :] = ref[...]
        at += ref.shape[0]


def join(blocks):
    height = sum(block.shape[0] for block in blocks)
    return pl.pallas_call(
        join_kernel,
        out_shape=jax.ShapeDtypeStruct((height, 128), BF16),
        in_specs=[VMEM] * len(blocks),
        out_specs=VMEM,
        compiler_params=SMALL,
    )(*blocks)


def exchange(value, axis, distance):
    size = lax.axis_size(axis)
    return lax.ppermute(value, axis, [(at, at ^ distance) for at in range(size)])


def after(value, *others):
    return lax.optimization_barrier((value, *others))[0]


def gather_and_finish(block, kept, rows, width):
    z2 = exchange(block, "dp", 8)
    z1 = exchange(block, "dp", 4)
    y0 = exchange(block, "dp", 2)
    beside = exchange(kept, "outer", 1)
    z2, beside = lax.optimization_barrier((z2, beside))
    z3 = exchange(z2, "dp", 4)
    y1 = exchange(z1, "dp", 2)
    y2 = exchange(z2, "dp", 2)
    y3 = exchange(z3, "dp", 2)
    near = [block, z1, z2]
    near = near + [exchange(v, "dp", 1) for v in near]
    gram = gram_of(near, rows, width)
    far = [y0, z3, y1, y2]
    far = far + [exchange(v, "dp", 1) for v in far]
    gram, last = lax.optimization_barrier((gram, y3))
    gram = gram_of(far, rows, width, gram)
    return finish(gram, block, [last, exchange(last, "dp", 1)], rows, width), beside


def away_kernel(grads_ref, away_ref, held, done):
    copy = pltpu.make_async_copy(grads_ref.at[1 - lax.axis_index("outer")], held, done)
    copy.start()
    copy.wait()
    pack(held[...].astype(BF16), away_ref)


def base_kernel(grads_ref, momentum_ref, kept_ref, base_ref, held, done):
    mine = lax.axis_index("outer")
    copies = [
        pltpu.make_async_copy(grads_ref.at[mine], held.at[0], done.at[0]),
        pltpu.make_async_copy(momentum_ref.at[mine], held.at[1], done.at[1]),
    ]
    for copy in copies:
        copy.start()
    for copy in copies:
        copy.wait()
    pack(held[0].astype(BF16), kept_ref)
    pack((1.0 + momentum_rate) * held[0] + (momentum_rate * momentum_rate) * held[1], base_ref)


def steering_kernel(base_ref, arrived_ref, out_ref):
    out_ref[...] = (base_ref[...] + (1.0 + momentum_rate) * arrived_ref[...].astype(F32)).astype(BF16)


def momentum_kernel(momentum_ref, kept_ref, arrived_ref, away_ref, arrived_too_ref, out_ref, held):
    mine = lax.axis_index("outer")
    rows, width = held.shape
    for at, sent, came in ((mine, kept_ref, arrived_ref), (1 - mine, away_ref, arrived_too_ref)):
        unpack(sent[...].astype(F32) + came[...].astype(F32), 0, held, 0, rows, width)
        out_ref[at] = momentum_rate * momentum_ref[at] + held[...]


def update_kernel(scale, own, rows_ref, *refs):
    out_ref, held, done = refs[-3:]
    mine = lax.axis_index("outer")
    unpack(scale * rows_ref[...].astype(F32), 0, held, 0, *held.shape)
    copy = pltpu.make_async_copy(held, out_ref.at[mine if own else 1 - mine], done)
    copy.start()
    copy.wait()


def two_pods(local, momentum):
    _, rows, width = local.shape
    update_scale = 0.2 * math.sqrt(max(rows * lax.axis_size("dp"), width))
    anywhere = pl.BlockSpec(memory_space=pl.ANY)
    one = (rows, width)
    packed = (rows * width // 128, 128)
    rounded = jax.ShapeDtypeStruct(packed, BF16)
    wide = jax.ShapeDtypeStruct(packed, F32)
    both = jax.ShapeDtypeStruct(local.shape, F32)
    away = pl.pallas_call(
        away_kernel,
        out_shape=rounded,
        in_specs=[anywhere],
        out_specs=VMEM,
        scratch_shapes=[pltpu.VMEM(one, F32), pltpu.SemaphoreType.DMA],
        compiler_params=SMALL,
    )(local)
    arrived = exchange(away, "outer", 1)
    kept, base = pl.pallas_call(
        base_kernel,
        out_shape=(rounded, wide),
        in_specs=[anywhere] * 2,
        out_specs=(VMEM, VMEM),
        scratch_shapes=[pltpu.VMEM((2,) + one, F32), pltpu.SemaphoreType.DMA((2,))],
        compiler_params=SMALL,
    )(local, momentum)
    steering = pl.pallas_call(
        steering_kernel, out_shape=rounded, in_specs=[VMEM] * 2, out_specs=VMEM, compiler_params=SMALL
    )(base, arrived)

    mine, arrived_too = gather_and_finish(steering, kept, rows, width)

    momentum_new = pl.pallas_call(
        momentum_kernel,
        out_shape=both,
        in_specs=[VMEM] * 5,
        scratch_shapes=[pltpu.VMEM(one, F32)],
        compiler_params=SMALL,
    )(momentum, kept, arrived, away, arrived_too)

    other = exchange(mine, "outer", 1)
    scratch = [pltpu.VMEM(one, F32), pltpu.SemaphoreType.DMA]
    half = pl.pallas_call(
        functools.partial(update_kernel, update_scale, True),
        out_shape=both,
        in_specs=[VMEM],
        out_specs=anywhere,
        scratch_shapes=scratch,
        compiler_params=SMALL,
    )(mine)
    update = pl.pallas_call(
        functools.partial(update_kernel, update_scale, False),
        out_shape=both,
        in_specs=[VMEM, anywhere],
        out_specs=anywhere,
        scratch_shapes=scratch,
        input_output_aliases={1: 0},
        compiler_params=SMALL,
    )(other, half)
    return momentum_new, update


def any_pods(local, momentum):
    pods = lax.axis_size("outer")
    pod = lax.axis_index("outer")
    count, rows, width = local.shape
    per_pod = count // pods
    update_scale = 0.2 * math.sqrt(max(rows * lax.axis_size("dp"), width))
    summed = lax.psum(local, "outer")
    momentum_new = momentum_rate * momentum + summed
    steering = summed + momentum_rate * momentum_new
    steering = lax.dynamic_slice_in_dim(steering, pod * per_pod, per_pod, 0).astype(BF16)
    mine = jnp.stack([whole_finish(steering[at]) for at in range(per_pod)])
    gathered = lax.all_gather(mine, "outer", axis=0, tiled=True)
    return momentum_new, update_scale * gathered.astype(F32)


def per_device(grads, momentum):
    local = grads[0]
    _, rows, width = local.shape
    halves = width % 128 == 64 and rows % 32 == 0
    if lax.axis_size("outer") == 2 and local.shape[0] == 2 and lax.axis_size("dp") == 16 and halves:
        return two_pods(local, momentum)
    return any_pods(local, momentum)


def solution(mesh):
    in_specs = (P("outer", None, "dp", None), P(None, "dp", None))
    out_specs = (P(None, "dp", None), P(None, "dp", None))
    return jax.shard_map(
        per_device, mesh=mesh, in_specs=in_specs, out_specs=out_specs, check_vma=False
    )
```

```python
import functools
import math

import jax
import jax.numpy as jnp
from jax import lax
from jax.experimental import pallas as pl
from jax.experimental.pallas import tpu as pltpu
from jax.sharding import PartitionSpec as P

ITERS = 2

coef_a = 3.4445
coef_b = -4.775
coef_c = 2.0315
momentum_rate = 0.95
epsilon = 1e-06

BF16 = jnp.bfloat16
F32 = jnp.float32
VMEM = pl.BlockSpec(memory_space=pltpu.VMEM)
SMEM = pl.BlockSpec(memory_space=pltpu.SMEM)
PARAMS = pltpu.CompilerParams(vmem_limit_bytes=16 * 1024 * 1024)
SMALL = pltpu.CompilerParams(vmem_limit_bytes=4 * 1024 * 1024)


def dot(left, right):
    return jnp.dot(left, right, preferred_element_type=F32)


def gram_product(matrix):
    return lax.dot_general(matrix, matrix, (((0,), (0,)), ((), ())), preferred_element_type=F32)


def trace_of(gram):
    size = gram.shape[0]
    total = jnp.zeros((1, 1), F32)
    for at in range(0, size, 128):
        part = min(128, size - at)
        block = gram[at : at + part, at : at + part]
        row = lax.broadcasted_iota(jnp.int32, (part, part), 0)
        column = lax.broadcasted_iota(jnp.int32, (part, part), 1)
        total = total + jnp.sum(jnp.where(row == column, block, 0.0), keepdims=True)
    return total


def own_rows(gram_raw, rows):
    gram = gram_raw.astype(BF16)
    squared = dot(gram, gram)
    inverse = 1.0 / (jnp.sqrt(trace_of(gram_raw)) + epsilon)
    scale = inverse * inverse
    polynomial = ((coef_b * scale) * gram.astype(F32) + (coef_c * scale * scale) * squared).astype(BF16)

    def by_q(value):
        return coef_a * value.astype(F32) + dot(value, polynomial)

    def by_second_gram(value):
        return by_q((scale * dot(by_q(value).astype(BF16), gram)).astype(BF16)).astype(BF16)

    first = by_q(rows)
    once = by_second_gram(first.astype(BF16))
    twice = by_second_gram(once)
    return inverse * (coef_a * first + coef_b * once.astype(F32) + coef_c * twice.astype(F32))


def pack(value, ref, at=0):
    rows, width = value.shape
    whole = width // 128
    for tile in range(whole):
        ref[at + rows * tile : at + rows * (tile + 1), :] = value[:, 128 * tile : 128 * (tile + 1)]
    rest = value[:, 128 * whole :]
    half = rows // 2
    ref[at + rows * whole : at + rows * whole + half, :] = jnp.concatenate([rest[:half], rest[half:]], axis=1)


def unpack(ref, at, held, to, rows, width):
    whole = width // 128
    for tile in range(whole):
        part = ref[at + rows * tile : at + rows * (tile + 1), :]
        held[to : to + rows, 128 * tile : 128 * (tile + 1)] = part.astype(held.dtype)
    half = rows // 2
    rest = ref[at + rows * whole : at + rows * whole + half, :].astype(held.dtype)
    held[to : to + half, 128 * whole :] = rest[:, :64]
    held[to + half : to + rows, 128 * whole :] = rest[:, 64:]


def unpack_all(blocks, held, rows, width):
    size = rows * width // 128
    to = 0
    for block in blocks:
        for at in range(0, block.shape[0], size):
            unpack(block, at, held, to, rows, width)
            to += rows
    return held[...]


def rows_in(blocks, width):
    return sum(block.shape[0] for block in blocks) * 128 // width


def gram_kernel(rows, more, *refs):
    blocks, out_ref, held = refs[more:-2], refs[-2], refs[-1]
    gram = gram_product(unpack_all(blocks, held, rows, held.shape[1]))
    out_ref[...] = refs[0][...] + gram if more else gram


def gram_of(blocks, rows, width, so_far=None):
    before = [] if so_far is None else [so_far]
    return pl.pallas_call(
        functools.partial(gram_kernel, rows, len(before)),
        out_shape=jax.ShapeDtypeStruct((width, width), F32),
        in_specs=[VMEM] * (len(before) + len(blocks)),
        out_specs=VMEM,
        scratch_shapes=[pltpu.VMEM((rows_in(blocks, width), width), BF16)],
        compiler_params=PARAMS,
    )(*before, *blocks)


def finish_kernel(rows, sum_ref, rows_ref, *refs):
    blocks, out_ref, held, own = refs[:-3], refs[-3], refs[-2], refs[-1]
    unpack(rows_ref, 0, own, 0, rows, own.shape[1])
    gram = sum_ref[...] + gram_product(unpack_all(blocks, held, rows, held.shape[1]))
    pack(own_rows(gram, own[...]).astype(BF16), out_ref)


def finish(so_far, own, blocks, rows, width):
    return pl.pallas_call(
        functools.partial(finish_kernel, rows),
        out_shape=jax.ShapeDtypeStruct(own.shape, BF16),
        in_specs=[VMEM] * (2 + len(blocks)),
        out_specs=VMEM,
        scratch_shapes=[pltpu.VMEM((rows_in(blocks, width), width), BF16), pltpu.VMEM((rows, width), BF16)],
        compiler_params=PARAMS,
    )(so_far, own, *blocks)


def whole_kernel(rows_ref, whole_ref, out_ref):
    out_ref[...] = own_rows(gram_product(whole_ref[...]), rows_ref[...]).astype(BF16)


def whole_finish(own):
    return pl.pallas_call(
        whole_kernel,
        out_shape=jax.ShapeDtypeStruct(own.shape, BF16),
        in_specs=[VMEM] * 2,
        out_specs=VMEM,
        compiler_params=PARAMS,
    )(own, lax.all_gather(own, "dp", axis=0, tiled=True))


def join_kernel(*refs):
    at = 0
    for ref in refs[:-1]:
        refs[-1][at : at + ref.shape[0], :] = ref[...]
        at += ref.shape[0]


def join(blocks):
    height = sum(block.shape[0] for block in blocks)
    return pl.pallas_call(
        join_kernel,
        out_shape=jax.ShapeDtypeStruct((height, 128), BF16),
        in_specs=[VMEM] * len(blocks),
        out_specs=VMEM,
        compiler_params=SMALL,
    )(*blocks)


def exchange(value, axis, distance):
    size = lax.axis_size(axis)
    return lax.ppermute(value, axis, [(at, at ^ distance) for at in range(size)])


def after(value, *others):
    return lax.optimization_barrier((value, *others))[0]


def gather_and_finish(block, kept, rows, width):
    z1 = exchange(block, "dp", 4)
    z2 = exchange(block, "dp", 8)
    y0 = exchange(block, "dp", 2)
    beside = exchange(kept, "outer", 1)
    z2, beside = lax.optimization_barrier((z2, beside))
    z3 = exchange(z2, "dp", 4)
    y2 = exchange(z2, "dp", 2)
    y1 = exchange(y0, "dp", 4)
    y3 = exchange(z3, "dp", 2)
    near = [block, z2, z1]
    near = near + [exchange(v, "dp", 1) for v in near]
    gram = gram_of(near, rows, width)
    far = [z3, y2, y0, y1]
    far = far + [exchange(v, "dp", 1) for v in far]
    gram, last = lax.optimization_barrier((gram, y3))
    gram = gram_of(far, rows, width, gram)
    return finish(gram, block, [last, exchange(last, "dp", 1)], rows, width), beside


def away_kernel(grads_ref, away_ref, held, done):
    copy = pltpu.make_async_copy(grads_ref.at[1 - lax.axis_index("outer")], held, done)
    copy.start()
    copy.wait()
    pack(held[...].astype(BF16), away_ref)


def base_kernel(grads_ref, momentum_ref, kept_ref, base_ref, held, done):
    mine = lax.axis_index("outer")
    copies = [
        pltpu.make_async_copy(grads_ref.at[mine], held.at[0], done.at[0]),
        pltpu.make_async_copy(momentum_ref.at[mine], held.at[1], done.at[1]),
    ]
    for copy in copies:
        copy.start()
    for copy in copies:
        copy.wait()
    pack(held[0].astype(BF16), kept_ref)
    pack((1.0 + momentum_rate) * held[0] + (momentum_rate * momentum_rate) * held[1], base_ref)


def steering_kernel(base_ref, arrived_ref, out_ref):
    out_ref[...] = (base_ref[...] + (1.0 + momentum_rate) * arrived_ref[...].astype(F32)).astype(BF16)


def momentum_kernel(momentum_ref, kept_ref, arrived_ref, away_ref, arrived_too_ref, out_ref, held):
    mine = lax.axis_index("outer")
    rows, width = held.shape
    for at, sent, came in ((mine, kept_ref, arrived_ref), (1 - mine, away_ref, arrived_too_ref)):
        unpack(sent[...].astype(F32) + came[...].astype(F32), 0, held, 0, rows, width)
        out_ref[at] = momentum_rate * momentum_ref[at] + held[...]


def update_kernel(scale, own, rows_ref, *refs):
    out_ref, held, done = refs[-3:]
    mine = lax.axis_index("outer")
    unpack(scale * rows_ref[...].astype(F32), 0, held, 0, *held.shape)
    copy = pltpu.make_async_copy(held, out_ref.at[mine if own else 1 - mine], done)
    copy.start()
    copy.wait()


def two_pods(local, momentum):
    _, rows, width = local.shape
    update_scale = 0.2 * math.sqrt(max(rows * lax.axis_size("dp"), width))
    anywhere = pl.BlockSpec(memory_space=pl.ANY)
    one = (rows, width)
    packed = (rows * width // 128, 128)
    rounded = jax.ShapeDtypeStruct(packed, BF16)
    wide = jax.ShapeDtypeStruct(packed, F32)
    both = jax.ShapeDtypeStruct(local.shape, F32)
    away = pl.pallas_call(
        away_kernel,
        out_shape=rounded,
        in_specs=[anywhere],
        out_specs=VMEM,
        scratch_shapes=[pltpu.VMEM(one, F32), pltpu.SemaphoreType.DMA],
        compiler_params=SMALL,
    )(local)
    arrived = exchange(away, "outer", 1)
    kept, base = pl.pallas_call(
        base_kernel,
        out_shape=(rounded, wide),
        in_specs=[anywhere] * 2,
        out_specs=(VMEM, VMEM),
        scratch_shapes=[pltpu.VMEM((2,) + one, F32), pltpu.SemaphoreType.DMA((2,))],
        compiler_params=SMALL,
    )(local, momentum)
    steering = pl.pallas_call(
        steering_kernel, out_shape=rounded, in_specs=[VMEM] * 2, out_specs=VMEM, compiler_params=SMALL
    )(base, arrived)

    mine, arrived_too = gather_and_finish(steering, kept, rows, width)

    momentum_new = pl.pallas_call(
        momentum_kernel,
        out_shape=both,
        in_specs=[VMEM] * 5,
        scratch_shapes=[pltpu.VMEM(one, F32)],
        compiler_params=SMALL,
    )(momentum, kept, arrived, away, arrived_too)

    other = exchange(mine, "outer", 1)
    scratch = [pltpu.VMEM(one, F32), pltpu.SemaphoreType.DMA]
    half = pl.pallas_call(
        functools.partial(update_kernel, update_scale, True),
        out_shape=both,
        in_specs=[VMEM],
        out_specs=anywhere,
        scratch_shapes=scratch,
        compiler_params=SMALL,
    )(mine)
    update = pl.pallas_call(
        functools.partial(update_kernel, update_scale, False),
        out_shape=both,
        in_specs=[VMEM, anywhere],
        out_specs=anywhere,
        scratch_shapes=scratch,
        input_output_aliases={1: 0},
        compiler_params=SMALL,
    )(other, half)
    return momentum_new, update


def any_pods(local, momentum):
    pods = lax.axis_size("outer")
    pod = lax.axis_index("outer")
    count, rows, width = local.shape
    per_pod = count // pods
    update_scale = 0.2 * math.sqrt(max(rows * lax.axis_size("dp"), width))
    summed = lax.psum(local, "outer")
    momentum_new = momentum_rate * momentum + summed
    steering = summed + momentum_rate * momentum_new
    steering = lax.dynamic_slice_in_dim(steering, pod * per_pod, per_pod, 0).astype(BF16)
    mine = jnp.stack([whole_finish(steering[at]) for at in range(per_pod)])
    gathered = lax.all_gather(mine, "outer", axis=0, tiled=True)
    return momentum_new, update_scale * gathered.astype(F32)


def per_device(grads, momentum):
    local = grads[0]
    _, rows, width = local.shape
    halves = width % 128 == 64 and rows % 32 == 0
    if lax.axis_size("outer") == 2 and local.shape[0] == 2 and lax.axis_size("dp") == 16 and halves:
        return two_pods(local, momentum)
    return any_pods(local, momentum)


def solution(mesh):
    in_specs = (P("outer", None, "dp", None), P(None, "dp", None))
    out_specs = (P(None, "dp", None), P(None, "dp", None))
    return jax.shard_map(
        per_device, mesh=mesh, in_specs=in_specs, out_specs=out_specs, check_vma=False
    )
```

```python
import functools
import math

import jax
import jax.numpy as jnp
from jax import lax
from jax.experimental import pallas as pl
from jax.experimental.pallas import tpu as pltpu
from jax.sharding import PartitionSpec as P

ITERS = 2

coef_a = 3.4445
coef_b = -4.775
coef_c = 2.0315
momentum_rate = 0.95
epsilon = 1e-06

BF16 = jnp.bfloat16
F32 = jnp.float32
VMEM = pl.BlockSpec(memory_space=pltpu.VMEM)
SMEM = pl.BlockSpec(memory_space=pltpu.SMEM)
PARAMS = pltpu.CompilerParams(vmem_limit_bytes=16 * 1024 * 1024)
SMALL = pltpu.CompilerParams(vmem_limit_bytes=4 * 1024 * 1024)


def dot(left, right):
    return jnp.dot(left, right, preferred_element_type=F32)


def gram_product(matrix):
    return lax.dot_general(matrix, matrix, (((0,), (0,)), ((), ())), preferred_element_type=F32)


def trace_of(gram):
    size = gram.shape[0]
    total = jnp.zeros((1, 1), F32)
    for at in range(0, size, 128):
        part = min(128, size - at)
        block = gram[at : at + part, at : at + part]
        row = lax.broadcasted_iota(jnp.int32, (part, part), 0)
        column = lax.broadcasted_iota(jnp.int32, (part, part), 1)
        total = total + jnp.sum(jnp.where(row == column, block, 0.0), keepdims=True)
    return total


def own_rows(gram_raw, rows):
    gram = gram_raw.astype(BF16)
    squared = dot(gram, gram)
    inverse = 1.0 / (jnp.sqrt(trace_of(gram_raw)) + epsilon)
    scale = inverse * inverse
    polynomial = ((coef_b * scale) * gram.astype(F32) + (coef_c * scale * scale) * squared).astype(BF16)

    def by_q(value):
        return coef_a * value.astype(F32) + dot(value, polynomial)

    def by_second_gram(value):
        return by_q((scale * dot(by_q(value).astype(BF16), gram)).astype(BF16)).astype(BF16)

    first = by_q(rows)
    once = by_second_gram(first.astype(BF16))
    twice = by_second_gram(once)
    return inverse * (coef_a * first + coef_b * once.astype(F32) + coef_c * twice.astype(F32))


def pack(value, ref, at=0):
    rows, width = value.shape
    whole = width // 128
    for tile in range(whole):
        ref[at + rows * tile : at + rows * (tile + 1), :] = value[:, 128 * tile : 128 * (tile + 1)]
    rest = value[:, 128 * whole :]
    half = rows // 2
    ref[at + rows * whole : at + rows * whole + half, :] = jnp.concatenate([rest[:half], rest[half:]], axis=1)


def unpack(ref, at, held, to, rows, width):
    whole = width // 128
    for tile in range(whole):
        part = ref[at + rows * tile : at + rows * (tile + 1), :]
        held[to : to + rows, 128 * tile : 128 * (tile + 1)] = part.astype(held.dtype)
    half = rows // 2
    rest = ref[at + rows * whole : at + rows * whole + half, :].astype(held.dtype)
    held[to : to + half, 128 * whole :] = rest[:, :64]
    held[to + half : to + rows, 128 * whole :] = rest[:, 64:]


def unpack_all(blocks, held, rows, width):
    size = rows * width // 128
    to = 0
    for block in blocks:
        for at in range(0, block.shape[0], size):
            unpack(block, at, held, to, rows, width)
            to += rows
    return held[...]


def rows_in(blocks, width):
    return sum(block.shape[0] for block in blocks) * 128 // width


def gram_kernel(rows, more, *refs):
    blocks, out_ref, held = refs[more:-2], refs[-2], refs[-1]
    gram = gram_product(unpack_all(blocks, held, rows, held.shape[1]))
    out_ref[...] = refs[0][...] + gram if more else gram


def gram_of(blocks, rows, width, so_far=None):
    before = [] if so_far is None else [so_far]
    return pl.pallas_call(
        functools.partial(gram_kernel, rows, len(before)),
        out_shape=jax.ShapeDtypeStruct((width, width), F32),
        in_specs=[VMEM] * (len(before) + len(blocks)),
        out_specs=VMEM,
        scratch_shapes=[pltpu.VMEM((rows_in(blocks, width), width), BF16)],
        compiler_params=PARAMS,
    )(*before, *blocks)


def finish_kernel(rows, sum_ref, rows_ref, *refs):
    blocks, out_ref, held, own = refs[:-3], refs[-3], refs[-2], refs[-1]
    unpack(rows_ref, 0, own, 0, rows, own.shape[1])
    gram = sum_ref[...] + gram_product(unpack_all(blocks, held, rows, held.shape[1]))
    pack(own_rows(gram, own[...]).astype(BF16), out_ref)


def finish(so_far, own, blocks, rows, width):
    return pl.pallas_call(
        functools.partial(finish_kernel, rows),
        out_shape=jax.ShapeDtypeStruct(own.shape, BF16),
        in_specs=[VMEM] * (2 + len(blocks)),
        out_specs=VMEM,
        scratch_shapes=[pltpu.VMEM((rows_in(blocks, width), width), BF16), pltpu.VMEM((rows, width), BF16)],
        compiler_params=PARAMS,
    )(so_far, own, *blocks)


def whole_kernel(rows_ref, whole_ref, out_ref):
    out_ref[...] = own_rows(gram_product(whole_ref[...]), rows_ref[...]).astype(BF16)


def whole_finish(own):
    return pl.pallas_call(
        whole_kernel,
        out_shape=jax.ShapeDtypeStruct(own.shape, BF16),
        in_specs=[VMEM] * 2,
        out_specs=VMEM,
        compiler_params=PARAMS,
    )(own, lax.all_gather(own, "dp", axis=0, tiled=True))


def join_kernel(*refs):
    at = 0
    for ref in refs[:-1]:
        refs[-1][at : at + ref.shape[0], :] = ref[...]
        at += ref.shape[0]


def join(blocks):
    height = sum(block.shape[0] for block in blocks)
    return pl.pallas_call(
        join_kernel,
        out_shape=jax.ShapeDtypeStruct((height, 128), BF16),
        in_specs=[VMEM] * len(blocks),
        out_specs=VMEM,
        compiler_params=SMALL,
    )(*blocks)


def exchange(value, axis, distance):
    size = lax.axis_size(axis)
    return lax.ppermute(value, axis, [(at, at ^ distance) for at in range(size)])


def after(value, *others):
    return lax.optimization_barrier((value, *others))[0]


def gather_and_finish(block, kept, rows, width):
    z2 = exchange(block, "dp", 8)
    z1 = exchange(block, "dp", 4)
    y0 = exchange(block, "dp", 2)
    beside = exchange(kept, "outer", 1)
    z2, beside = lax.optimization_barrier((z2, beside))
    z3 = exchange(z2, "dp", 4)
    y1 = exchange(z1, "dp", 2)
    y2 = exchange(z2, "dp", 2)
    y3 = exchange(z3, "dp", 2)
    near = [block, z1, z2]
    near = near + [exchange(v, "dp", 1) for v in near]
    gram = gram_of(near, rows, width)
    far = [y0, z3, y1, y2]
    far = far + [exchange(v, "dp", 1) for v in far]
    gram, last = lax.optimization_barrier((gram, y3))
    gram = gram_of(far, rows, width, gram)
    return finish(gram, block, [last, exchange(last, "dp", 1)], rows, width), beside


def away_kernel(grads_ref, away_ref):
    pack(grads_ref[1 - lax.axis_index("outer")].astype(BF16), away_ref)


def base_kernel(grads_ref, momentum_ref, kept_ref, base_ref, held, done):
    mine = lax.axis_index("outer")
    copies = [
        pltpu.make_async_copy(grads_ref.at[mine], held.at[0], done.at[0]),
        pltpu.make_async_copy(momentum_ref.at[mine], held.at[1], done.at[1]),
    ]
    for copy in copies:
        copy.start()
    for copy in copies:
        copy.wait()
    pack(held[0].astype(BF16), kept_ref)
    pack((1.0 + momentum_rate) * held[0] + (momentum_rate * momentum_rate) * held[1], base_ref)


def steering_kernel(base_ref, arrived_ref, out_ref):
    out_ref[...] = (base_ref[...] + (1.0 + momentum_rate) * arrived_ref[...].astype(F32)).astype(BF16)


def momentum_kernel(momentum_ref, kept_ref, arrived_ref, away_ref, arrived_too_ref, out_ref, held):
    mine = lax.axis_index("outer")
    rows, width = held.shape
    for at, sent, came in ((mine, kept_ref, arrived_ref), (1 - mine, away_ref, arrived_too_ref)):
        unpack(sent[...].astype(F32) + came[...].astype(F32), 0, held, 0, rows, width)
        out_ref[at] = momentum_rate * momentum_ref[at] + held[...]


def update_kernel(scale, own, rows_ref, *refs):
    out_ref, held, done = refs[-3:]
    mine = lax.axis_index("outer")
    unpack(scale * rows_ref[...].astype(F32), 0, held, 0, *held.shape)
    copy = pltpu.make_async_copy(held, out_ref.at[mine if own else 1 - mine], done)
    copy.start()
    copy.wait()


def two_pods(local, momentum):
    _, rows, width = local.shape
    update_scale = 0.2 * math.sqrt(max(rows * lax.axis_size("dp"), width))
    anywhere = pl.BlockSpec(memory_space=pl.ANY)
    one = (rows, width)
    packed = (rows * width // 128, 128)
    rounded = jax.ShapeDtypeStruct(packed, BF16)
    wide = jax.ShapeDtypeStruct(packed, F32)
    both = jax.ShapeDtypeStruct(local.shape, F32)
    away = pl.pallas_call(
        away_kernel,
        out_shape=rounded,
        in_specs=[VMEM],
        out_specs=VMEM,
        compiler_params=SMALL,
    )(local)
    arrived = exchange(away, "outer", 1)
    kept, base = pl.pallas_call(
        base_kernel,
        out_shape=(rounded, wide),
        in_specs=[anywhere] * 2,
        out_specs=(VMEM, VMEM),
        scratch_shapes=[pltpu.VMEM((2,) + one, F32), pltpu.SemaphoreType.DMA((2,))],
        compiler_params=SMALL,
    )(local, momentum)
    steering = pl.pallas_call(
        steering_kernel, out_shape=rounded, in_specs=[VMEM] * 2, out_specs=VMEM, compiler_params=SMALL
    )(base, arrived)

    mine, arrived_too = gather_and_finish(steering, kept, rows, width)

    momentum_new = pl.pallas_call(
        momentum_kernel,
        out_shape=both,
        in_specs=[VMEM] * 5,
        scratch_shapes=[pltpu.VMEM(one, F32)],
        compiler_params=SMALL,
    )(momentum, kept, arrived, away, arrived_too)

    other = exchange(mine, "outer", 1)
    scratch = [pltpu.VMEM(one, F32), pltpu.SemaphoreType.DMA]
    half = pl.pallas_call(
        functools.partial(update_kernel, update_scale, True),
        out_shape=both,
        in_specs=[VMEM],
        out_specs=anywhere,
        scratch_shapes=scratch,
        compiler_params=SMALL,
    )(mine)
    update = pl.pallas_call(
        functools.partial(update_kernel, update_scale, False),
        out_shape=both,
        in_specs=[VMEM, anywhere],
        out_specs=anywhere,
        scratch_shapes=scratch,
        input_output_aliases={1: 0},
        compiler_params=SMALL,
    )(other, half)
    return momentum_new, update


def any_pods(local, momentum):
    pods = lax.axis_size("outer")
    pod = lax.axis_index("outer")
    count, rows, width = local.shape
    per_pod = count // pods
    update_scale = 0.2 * math.sqrt(max(rows * lax.axis_size("dp"), width))
    summed = lax.psum(local, "outer")
    momentum_new = momentum_rate * momentum + summed
    steering = summed + momentum_rate * momentum_new
    steering = lax.dynamic_slice_in_dim(steering, pod * per_pod, per_pod, 0).astype(BF16)
    mine = jnp.stack([whole_finish(steering[at]) for at in range(per_pod)])
    gathered = lax.all_gather(mine, "outer", axis=0, tiled=True)
    return momentum_new, update_scale * gathered.astype(F32)


def per_device(grads, momentum):
    local = grads[0]
    _, rows, width = local.shape
    halves = width % 128 == 64 and rows % 32 == 0
    if lax.axis_size("outer") == 2 and local.shape[0] == 2 and lax.axis_size("dp") == 16 and halves:
        return two_pods(local, momentum)
    return any_pods(local, momentum)


def solution(mesh):
    in_specs = (P("outer", None, "dp", None), P(None, "dp", None))
    out_specs = (P(None, "dp", None), P(None, "dp", None))
    return jax.shard_map(
        per_device, mesh=mesh, in_specs=in_specs, out_specs=out_specs, check_vma=False
    )
```

```python
import functools
import math

import jax
import jax.numpy as jnp
from jax import lax
from jax.experimental import pallas as pl
from jax.experimental.pallas import tpu as pltpu
from jax.sharding import PartitionSpec as P

ITERS = 2

coef_a = 3.4445
coef_b = -4.775
coef_c = 2.0315
momentum_rate = 0.95
epsilon = 1e-06

BF16 = jnp.bfloat16
F32 = jnp.float32
VMEM = pl.BlockSpec(memory_space=pltpu.VMEM)
SMEM = pl.BlockSpec(memory_space=pltpu.SMEM)
PARAMS = pltpu.CompilerParams(vmem_limit_bytes=16 * 1024 * 1024)
SMALL = pltpu.CompilerParams(vmem_limit_bytes=4 * 1024 * 1024)


def dot(left, right):
    return jnp.dot(left, right, preferred_element_type=F32)


def gram_product(matrix):
    return lax.dot_general(matrix, matrix, (((0,), (0,)), ((), ())), preferred_element_type=F32)


def trace_of(gram):
    size = gram.shape[0]
    total = jnp.zeros((1, 1), F32)
    for at in range(0, size, 128):
        part = min(128, size - at)
        block = gram[at : at + part, at : at + part]
        row = lax.broadcasted_iota(jnp.int32, (part, part), 0)
        column = lax.broadcasted_iota(jnp.int32, (part, part), 1)
        total = total + jnp.sum(jnp.where(row == column, block, 0.0), keepdims=True)
    return total


def own_rows(gram_raw, rows):
    gram = gram_raw.astype(BF16)
    squared = dot(gram, gram)
    inverse = 1.0 / (jnp.sqrt(trace_of(gram_raw)) + epsilon)
    scale = inverse * inverse
    polynomial = ((coef_b * scale) * gram.astype(F32) + (coef_c * scale * scale) * squared).astype(BF16)

    def by_q(value):
        return coef_a * value.astype(F32) + dot(value, polynomial)

    def by_second_gram(value):
        return by_q((scale * dot(by_q(value).astype(BF16), gram)).astype(BF16)).astype(BF16)

    first = by_q(rows)
    once = by_second_gram(first.astype(BF16))
    twice = by_second_gram(once)
    return inverse * (coef_a * first + coef_b * once.astype(F32) + coef_c * twice.astype(F32))


def pack(value, ref, at=0):
    rows, width = value.shape
    whole = width // 128
    for tile in range(whole):
        ref[at + rows * tile : at + rows * (tile + 1), :] = value[:, 128 * tile : 128 * (tile + 1)]
    rest = value[:, 128 * whole :]
    half = rows // 2
    ref[at + rows * whole : at + rows * whole + half, :] = jnp.concatenate([rest[:half], rest[half:]], axis=1)


def unpack(ref, at, held, to, rows, width):
    whole = width // 128
    for tile in range(whole):
        part = ref[at + rows * tile : at + rows * (tile + 1), :]
        held[to : to + rows, 128 * tile : 128 * (tile + 1)] = part.astype(held.dtype)
    half = rows // 2
    rest = ref[at + rows * whole : at + rows * whole + half, :].astype(held.dtype)
    held[to : to + half, 128 * whole :] = rest[:, :64]
    held[to + half : to + rows, 128 * whole :] = rest[:, 64:]


def unpack_all(blocks, held, rows, width):
    size = rows * width // 128
    to = 0
    for block in blocks:
        for at in range(0, block.shape[0], size):
            unpack(block, at, held, to, rows, width)
            to += rows
    return held[...]


def rows_in(blocks, width):
    return sum(block.shape[0] for block in blocks) * 128 // width


def gram_kernel(rows, more, *refs):
    blocks, out_ref, held = refs[more:-2], refs[-2], refs[-1]
    gram = gram_product(unpack_all(blocks, held, rows, held.shape[1]))
    out_ref[...] = refs[0][...] + gram if more else gram


def gram_of(blocks, rows, width, so_far=None):
    before = [] if so_far is None else [so_far]
    return pl.pallas_call(
        functools.partial(gram_kernel, rows, len(before)),
        out_shape=jax.ShapeDtypeStruct((width, width), F32),
        in_specs=[VMEM] * (len(before) + len(blocks)),
        out_specs=VMEM,
        scratch_shapes=[pltpu.VMEM((rows_in(blocks, width), width), BF16)],
        compiler_params=PARAMS,
    )(*before, *blocks)


def finish_kernel(rows, sum_ref, rows_ref, *refs):
    blocks, out_ref, held, own = refs[:-3], refs[-3], refs[-2], refs[-1]
    unpack(rows_ref, 0, own, 0, rows, own.shape[1])
    gram = sum_ref[...] + gram_product(unpack_all(blocks, held, rows, held.shape[1]))
    pack(own_rows(gram, own[...]).astype(BF16), out_ref)


def finish(so_far, own, blocks, rows, width):
    return pl.pallas_call(
        functools.partial(finish_kernel, rows),
        out_shape=jax.ShapeDtypeStruct(own.shape, BF16),
        in_specs=[VMEM] * (2 + len(blocks)),
        out_specs=VMEM,
        scratch_shapes=[pltpu.VMEM((rows_in(blocks, width), width), BF16), pltpu.VMEM((rows, width), BF16)],
        compiler_params=PARAMS,
    )(so_far, own, *blocks)


def whole_kernel(rows_ref, whole_ref, out_ref):
    out_ref[...] = own_rows(gram_product(whole_ref[...]), rows_ref[...]).astype(BF16)


def whole_finish(own):
    return pl.pallas_call(
        whole_kernel,
        out_shape=jax.ShapeDtypeStruct(own.shape, BF16),
        in_specs=[VMEM] * 2,
        out_specs=VMEM,
        compiler_params=PARAMS,
    )(own, lax.all_gather(own, "dp", axis=0, tiled=True))


def join_kernel(*refs):
    at = 0
    for ref in refs[:-1]:
        refs[-1][at : at + ref.shape[0], :] = ref[...]
        at += ref.shape[0]


def join(blocks):
    height = sum(block.shape[0] for block in blocks)
    return pl.pallas_call(
        join_kernel,
        out_shape=jax.ShapeDtypeStruct((height, 128), BF16),
        in_specs=[VMEM] * len(blocks),
        out_specs=VMEM,
        compiler_params=SMALL,
    )(*blocks)


def exchange(value, axis, distance):
    size = lax.axis_size(axis)
    return lax.ppermute(value, axis, [(at, at ^ distance) for at in range(size)])


def after(value, *others):
    return lax.optimization_barrier((value, *others))[0]


def gather_and_finish(block, kept, rows, width):
    z2 = exchange(block, "dp", 8)
    z1 = exchange(block, "dp", 4)
    y0 = exchange(block, "dp", 2)
    beside = exchange(kept, "outer", 1)
    z2, beside = lax.optimization_barrier((z2, beside))
    z3 = exchange(z2, "dp", 4)
    y1 = exchange(z1, "dp", 2)
    y2 = exchange(z2, "dp", 2)
    y3 = exchange(z3, "dp", 2)
    near = [block, z1, z2]
    near = near + [exchange(v, "dp", 1) for v in near]
    gram = gram_of(near, rows, width)
    far = [y0, z3, y1, y2]
    far = far + [exchange(v, "dp", 1) for v in far]
    gram, last = lax.optimization_barrier((gram, y3))
    gram = gram_of(far, rows, width, gram)
    return finish(gram, block, [last, exchange(last, "dp", 1)], rows, width), beside


def away_kernel(grads_ref, away_ref):
    pack(grads_ref[1 - lax.axis_index("outer")].astype(BF16), away_ref)


def base_kernel(grads_ref, momentum_ref, kept_ref, base_ref, held, done):
    mine = lax.axis_index("outer")
    copies = [
        pltpu.make_async_copy(grads_ref.at[mine], held.at[0], done.at[0]),
        pltpu.make_async_copy(momentum_ref.at[mine], held.at[1], done.at[1]),
    ]
    for copy in copies:
        copy.start()
    for copy in copies:
        copy.wait()
    pack(held[0].astype(BF16), kept_ref)
    pack((1.0 + momentum_rate) * held[0] + (momentum_rate * momentum_rate) * held[1], base_ref)


def steering_kernel(base_ref, arrived_ref, out_ref):
    out_ref[...] = (base_ref[...] + (1.0 + momentum_rate) * arrived_ref[...].astype(F32)).astype(BF16)


def momentum_kernel(momentum_ref, kept_ref, arrived_ref, away_ref, arrived_too_ref, out_ref, held):
    mine = lax.axis_index("outer")
    rows, width = held.shape
    for at, sent, came in ((mine, kept_ref, arrived_ref), (1 - mine, away_ref, arrived_too_ref)):
        unpack(sent[...].astype(F32) + came[...].astype(F32), 0, held, 0, rows, width)
        out_ref[at] = momentum_rate * momentum_ref[at] + held[...]


def update_kernel(scale, own, rows_ref, *refs):
    out_ref, held, done = refs[-3:]
    rows, width = held.shape
    whole = width // 128
    half = rows // 2
    mine = lax.axis_index("outer")
    target = out_ref.at[mine if own else 1 - mine]
    copies = []
    for part in range(2):
        at = half * part
        for tile in range(whole):
            block = rows_ref[rows * tile + at : rows * tile + at + half, :].astype(F32)
            held[at : at + half, 128 * tile : 128 * (tile + 1)] = scale * block
        rest = rows_ref[rows * whole : rows * whole + half, :].astype(F32)
        held[at : at + half, 128 * whole :] = scale * rest[:, 64 * part : 64 * (part + 1)]
        span = pl.ds(at, half)
        copies.append(pltpu.make_async_copy(held.at[span], target.at[span], done.at[part]))
        copies[-1].start()
    for copy in copies:
        copy.wait()


def two_pods(local, momentum):
    _, rows, width = local.shape
    update_scale = 0.2 * math.sqrt(max(rows * lax.axis_size("dp"), width))
    anywhere = pl.BlockSpec(memory_space=pl.ANY)
    one = (rows, width)
    packed = (rows * width // 128, 128)
    rounded = jax.ShapeDtypeStruct(packed, BF16)
    wide = jax.ShapeDtypeStruct(packed, F32)
    both = jax.ShapeDtypeStruct(local.shape, F32)
    away = pl.pallas_call(
        away_kernel,
        out_shape=rounded,
        in_specs=[VMEM],
        out_specs=VMEM,
        compiler_params=SMALL,
    )(local)
    arrived = exchange(away, "outer", 1)
    kept, base = pl.pallas_call(
        base_kernel,
        out_shape=(rounded, wide),
        in_specs=[anywhere] * 2,
        out_specs=(VMEM, VMEM),
        scratch_shapes=[pltpu.VMEM((2,) + one, F32), pltpu.SemaphoreType.DMA((2,))],
        compiler_params=SMALL,
    )(local, momentum)
    steering = pl.pallas_call(
        steering_kernel, out_shape=rounded, in_specs=[VMEM] * 2, out_specs=VMEM, compiler_params=SMALL
    )(base, arrived)

    mine, arrived_too = gather_and_finish(steering, kept, rows, width)

    momentum_new = pl.pallas_call(
        momentum_kernel,
        out_shape=both,
        in_specs=[VMEM] * 5,
        scratch_shapes=[pltpu.VMEM(one, F32)],
        compiler_params=SMALL,
    )(momentum, kept, arrived, away, arrived_too)

    other = exchange(mine, "outer", 1)
    scratch = [pltpu.VMEM(one, F32), pltpu.SemaphoreType.DMA((2,))]
    half = pl.pallas_call(
        functools.partial(update_kernel, update_scale, True),
        out_shape=both,
        in_specs=[VMEM],
        out_specs=anywhere,
        scratch_shapes=scratch,
        compiler_params=SMALL,
    )(mine)
    update = pl.pallas_call(
        functools.partial(update_kernel, update_scale, False),
        out_shape=both,
        in_specs=[VMEM, anywhere],
        out_specs=anywhere,
        scratch_shapes=scratch,
        input_output_aliases={1: 0},
        compiler_params=SMALL,
    )(other, half)
    return momentum_new, update


def any_pods(local, momentum):
    pods = lax.axis_size("outer")
    pod = lax.axis_index("outer")
    count, rows, width = local.shape
    per_pod = count // pods
    update_scale = 0.2 * math.sqrt(max(rows * lax.axis_size("dp"), width))
    summed = lax.psum(local, "outer")
    momentum_new = momentum_rate * momentum + summed
    steering = summed + momentum_rate * momentum_new
    steering = lax.dynamic_slice_in_dim(steering, pod * per_pod, per_pod, 0).astype(BF16)
    mine = jnp.stack([whole_finish(steering[at]) for at in range(per_pod)])
    gathered = lax.all_gather(mine, "outer", axis=0, tiled=True)
    return momentum_new, update_scale * gathered.astype(F32)


def per_device(grads, momentum):
    local = grads[0]
    _, rows, width = local.shape
    halves = width % 128 == 64 and rows % 32 == 0
    if lax.axis_size("outer") == 2 and local.shape[0] == 2 and lax.axis_size("dp") == 16 and halves:
        return two_pods(local, momentum)
    return any_pods(local, momentum)


def solution(mesh):
    in_specs = (P("outer", None, "dp", None), P(None, "dp", None))
    out_specs = (P(None, "dp", None), P(None, "dp", None))
    return jax.shard_map(
        per_device, mesh=mesh, in_specs=in_specs, out_specs=out_specs, check_vma=False
    )
```
